32 devices in a mesh: dp: 4 (over y, x), expert: 8 (over z, core).
Axes of the slice: x: 2, y: 2, z: 4, core: 2. Of those that a mesh axis runs over, the one named last changes fastest.
Arguments:
- tokens: bfloat16 [4096, 4096], P(('dp', 'expert')), may hold values from -6 to 6
- cotangent: bfloat16 [4096, 4096], P(('dp', 'expert')), may hold values from -25 to 25
- routes: int32 [4096, 2], P(('dp', 'expert')), may hold values from 0 to 7, all different within a row; in each aligned block of 128 rows (0 to 127, 128 to 255, ...) at most 64 rows name the same one
- route_gates: float32 [4096, 2], P(('dp', 'expert')), may hold values from 0.2 to 1
- norm_gain: float32 [4096], replicated, may hold values from 0.25 to 1.75
- gate_matrix: bfloat16 [8, 4096, 768], P('expert'), may hold values from -0.140625 to 0.140625
- up_matrix: bfloat16 [8, 4096, 768], P('expert'), may hold values from -0.140625 to 0.140625
- down_matrix: bfloat16 [8, 4096, 768], P('expert'), may hold values from -0.21650635 to 0.21650635
Outputs:
- input_grad: bfloat16 [4096, 4096], P(('dp', 'expert'))
- gain_grad: float32 [4096], P(('dp', 'expert'))
The draws below stay inside these ranges and needn't reach their ends.
Inputs may be any that keep to these rules, and one draw needn't show every extreme that they name: `routes`: each row names 2 different experts. In the rows of one device no expert is named more than 64 times, and in every draw some device's rows name some expert exactly 64 times.
All inputs are finite; a program needn't handle non-finite values.
Results may differ from the reference program's by a relative error of at most 0.0057.
Values may be sent and summed in bfloat16 or wider, within the bound.
No kernel may reach another device: no remote copies, remote signals or barrier semaphores. Data moves between devices by JAX's collectives and lax.ppermute only.
A program may use at most 128 MiB of HBM per device.

```python
import math
import jax
import jax.numpy as jnp
import numpy as np
from jax import lax

D = 4096
FF = 768
TOPW = 2
TOK_DEV = 128
EXPERTS = 8
CAP = 64
TOKENS = 4096


def input_field(key):
    field_key = jax.random.fold_in(key, 1)
    values = jnp.clip(jax.random.normal(field_key, (TOKENS, D), jnp.float32), -6.0, 6.0)
    return values


def draw_tokens(key, part):
    return input_field(key).astype(jnp.bfloat16)


def draw_cotangent(key, part):
    field = input_field(key)
    sign_bits = jax.random.randint(jax.random.fold_in(key, 3), (TOKENS, 1), 0, 2)
    signs = (2 * sign_bits - 1).astype(jnp.float32)
    noise_key = jax.random.fold_in(key, 2)
    noise = jnp.clip(jax.random.normal(noise_key, (TOKENS, D), jnp.float32), -4.0, 4.0)
    blocks = TOKENS // TOK_DEV
    width = D // blocks
    pairing = jax.random.permutation(jax.random.fold_in(key, 4), blocks).astype(jnp.int32)
    boost = jnp.where(pairing[:, None] == jnp.arange(blocks, dtype=jnp.int32)[None, :], 4.0, 1.0).astype(jnp.float32)
    noise = (noise.reshape(blocks, TOK_DEV, blocks, width) * boost[:, None, :, None]).reshape(TOKENS, D)
    return (signs * 1.5 * field + noise).astype(jnp.bfloat16)


def expert_stack(key, own_tag, scale):
    own_key = jax.random.fold_in(key, own_tag)
    shared_key = jax.random.fold_in(key, own_tag + 1)
    shared = jnp.clip(jax.random.normal(shared_key, (D, FF), jnp.float32), -4.0, 4.0)
    own = jnp.clip(jax.random.normal(own_key, (EXPERTS, D, FF), jnp.float32), -4.0, 4.0)
    return ((shared[None, :, :] + 0.5 * own) * (scale / math.sqrt(1.25))).astype(jnp.bfloat16)


def draw_gate_matrix(key, part):
    return expert_stack(key, 101, 1.5 / math.sqrt(D))


def draw_up_matrix(key, part):
    return expert_stack(key, 201, 1.5 / math.sqrt(D))


def draw_down_matrix(key, part):
    return expert_stack(key, 301, 1.0 / math.sqrt(FF))


def block_scale(key, dims, split, least, high):
    def one(dim, blocks):
        heights = jax.random.uniform(jax.random.fold_in(jax.random.fold_in(key, 6), dim), (blocks,), jnp.float32, least / len(split), high / len(split))
        return jnp.repeat(jnp.exp(heights), dims[dim] // blocks).reshape((-1,) + (1,) * (len(dims) - dim - 1))

    gain = one(*split[0])
    for cut in split[1:]:
        gain = gain * one(*cut)
    return gain


def deal_out(key, own, number, rows, count, top, most, skew):
    sequence = jax.random.permutation(key, count)
    packed, ordinary = portions_of(count, rows * top, most, skew, True), portions_of(count, rows * top, most, skew, False)
    places = jnp.arange(count)

    def named(sizes, offset_by):
        used = int((sizes > 0).sum())
        fixed = max(1, used // 4)
        shifted = fixed + (places - fixed + offset_by * (used - fixed)) % max(1, count - fixed)
        return jnp.zeros((count,), jnp.int32).at[sequence[jnp.where(places < fixed, places, shifted)]].set(jnp.asarray(sizes, jnp.int32))

    sizes = jnp.where(number % 4 == 0, named(packed, number // 4), named(ordinary, number - number // 4 - 1))
    mixed = jax.random.permutation(jax.random.fold_in(own, 3), count)
    source_of, sink = mixed[0:count // 2 * 2:2], mixed[1:count // 2 * 2:2]
    margin = jnp.minimum(sizes[source_of] - 1, most - sizes[sink]) // 2
    margin = jnp.where((source_of == sequence[0]) | (sink == sequence[0]) | (sizes[sink] == 0), 0, jnp.maximum(margin, 0))
    shifted = jax.random.randint(jax.random.fold_in(own, 4), (count // 2,), 0, 1 << 20) % (margin + 1)
    sizes = sizes.at[source_of].add(-shifted).at[sink].add(shifted)
    labels = jnp.searchsorted(jnp.cumsum(sizes), jnp.arange(rows * top), side="right").astype(jnp.int32)
    table = labels.reshape(top, rows).T
    table = table[jax.random.permutation(jax.random.fold_in(own, 1), rows)]
    offset_by = jax.random.randint(jax.random.fold_in(own, 2), (rows, 1), 0, top)
    return jnp.take_along_axis(table, (jnp.arange(top)[None, :] + offset_by) % top, axis=1)


def portions_of(amount, total, most, lean, full):
    loads = [(1 << 20) // math.isqrt(grade ** lean) + 1 for grade in range(1, amount + 1)]
    largest = most if full else min(most, max(-(-total // amount), total * loads[0] // sum(loads)))
    least = 1 if total - largest >= amount - 1 else 0
    counts, spare = [largest] + [least] * (amount - 1), total - largest - least * (amount - 1)
    while spare > 0:
        movable = [i for i in range(1, amount) if counts[i] < largest] or [i for i in range(1, amount) if counts[i] < most]
        pool, budget = sum([loads[i] for i in movable]), spare
        for i in movable:
            more = min(most - counts[i], max(1, budget * loads[i] // pool), spare)
            counts[i] = counts[i] + more
            spare = spare - more
    return np.array(counts)


def setup_inputs(seed: int = 0) -> dict:
    seeds = jax.random.split(jax.random.key(seed), 9)
    tokens = draw_tokens(jax.random.fold_in(seeds[8], 71), 0)
    cotangent = draw_cotangent(jax.random.fold_in(seeds[8], 71), 0)
    routes_keys = jax.random.split(jax.random.fold_in(seeds[2], 1), TOKENS // TOK_DEV)
    routes_turns = jax.random.permutation(jax.random.fold_in(seeds[2], 3), TOKENS // TOK_DEV)
    routes = jax.vmap(lambda own, number: deal_out(jax.random.fold_in(seeds[2], 2), own, number, TOK_DEV, EXPERTS, TOPW, CAP, 2))(routes_keys, routes_turns).reshape((TOKENS, TOPW))
    route_gates = jnp.clip(jnp.exp(math.log(1.0) - 1.609438 * jax.random.uniform(seeds[3], (TOKENS, TOPW), jnp.float32) ** block_scale(seeds[3], (TOKENS, TOPW), ((0, 32),), -0.2, 0.2)), 0.2, 1.0)
    norm_gain = jnp.clip(1.0 + 0.15 * jax.random.normal(seeds[4], (D,), jnp.float32), 0.25, 1.75)
    gate_matrix = draw_gate_matrix(jax.random.fold_in(seeds[8], 71), 0)
    up_matrix = draw_up_matrix(jax.random.fold_in(seeds[8], 71), 0)
    down_matrix = draw_down_matrix(jax.random.fold_in(seeds[8], 71), 0)
    return {"tokens": tokens, "cotangent": cotangent, "routes": routes, "route_gates": route_gates, "norm_gain": norm_gain, "gate_matrix": gate_matrix, "up_matrix": up_matrix, "down_matrix": down_matrix}


def reference(tokens, cotangent, routes, route_gates, norm_gain, gate_matrix, up_matrix, down_matrix):
    token_count = tokens.shape[0]
    features = tokens.shape[1]
    top_routes = routes.shape[1]
    experts = gate_matrix.shape[0]
    blocks = token_count // TOK_DEV
    flat_ids = routes.reshape(blocks, TOK_DEV * top_routes)
    onehot = (flat_ids[:, :, None] == jnp.arange(experts, dtype=jnp.int32)[None, None, :]).astype(jnp.int32)
    before = jnp.cumsum(onehot, axis=1) - onehot
    ranks = lax.optimization_barrier(jnp.sum(before * onehot, axis=2))
    slot_of = (jnp.arange(blocks, dtype=jnp.int32)[:, None] * CAP + ranks).reshape(-1).astype(jnp.int32)
    owner_ids = routes.reshape(-1).astype(jnp.int32)
    token_of = jnp.repeat(jnp.arange(token_count, dtype=jnp.int32), top_routes)
    slot_count = blocks * CAP
    slot_token = jnp.full((experts, slot_count), token_count, dtype=jnp.int32).at[owner_ids, slot_of].set(token_of)
    slot_gate = jnp.zeros((experts, slot_count), jnp.float32).at[owner_ids, slot_of].set(route_gates.reshape(-1))
    padded_tokens = jnp.concatenate([tokens, jnp.zeros((1, features), tokens.dtype)], axis=0)

    def project(slot_rows, gate_local, up_local):
        expert_rows = padded_tokens[slot_rows]
        pre_gate = jnp.dot(expert_rows, gate_local, preferred_element_type=jnp.float32)
        pre_up = jnp.dot(expert_rows, up_local, preferred_element_type=jnp.float32)
        return (pre_gate, pre_up)

    def forward(combined, inputs):
        slot_rows, route_scale, gate_local, up_local, down_local = inputs
        pre_gate, pre_up = project(slot_rows, gate_local, up_local)
        sigmoid_gate = jax.nn.sigmoid(pre_gate)
        hidden = (pre_gate * sigmoid_gate * pre_up).astype(jnp.bfloat16)
        expert_out = lax.dot_general(hidden, down_local, (((1,), (1,)), ((), ())), preferred_element_type=jnp.float32).astype(jnp.bfloat16)
        return (combined.at[slot_rows].add(route_scale[:, None] * expert_out.astype(jnp.float32)), None)
    combined, _ = lax.scan(forward, jnp.zeros((token_count + 1, features), jnp.float32), (slot_token, slot_gate, gate_matrix, up_matrix, down_matrix))
    residual = tokens.astype(jnp.float32) + combined[:token_count]
    inverse_rms = lax.rsqrt(lax.optimization_barrier(jnp.mean(residual * residual, axis=1, keepdims=True)) + 1e-06)
    normed = residual * inverse_rms
    upstream = cotangent.astype(jnp.float32)
    gain_grad = lax.optimization_barrier(jnp.sum(upstream * normed, axis=0))
    scaled = upstream * norm_gain[None, :]
    resid_grad = inverse_rms * (scaled - normed * lax.optimization_barrier(jnp.mean(scaled * normed, axis=1, keepdims=True)))
    padded_grad = jnp.concatenate([resid_grad, jnp.zeros((1, features), jnp.float32)], axis=0)

    def backward(grad_sum, inputs):
        slot_rows, route_scale, gate_local, up_local, down_local = inputs
        pre_gate, pre_up = project(slot_rows, gate_local, up_local)
        sigmoid_gate = jax.nn.sigmoid(pre_gate)
        route_grad = (route_scale[:, None] * padded_grad[slot_rows]).astype(jnp.bfloat16)
        hidden_grad = jnp.dot(route_grad, down_local, preferred_element_type=jnp.float32)
        gate_grad = (hidden_grad * pre_up * sigmoid_gate * (1.0 + pre_gate * (1.0 - sigmoid_gate))).astype(jnp.bfloat16)
        up_grad = (hidden_grad * pre_gate * sigmoid_gate).astype(jnp.bfloat16)
        row_grad = lax.dot_general(gate_grad, gate_local, (((1,), (1,)), ((), ())), preferred_element_type=jnp.float32)
        row_grad = row_grad + lax.dot_general(up_grad, up_local, (((1,), (1,)), ((), ())), preferred_element_type=jnp.float32)
        row_grad = row_grad.astype(jnp.bfloat16)
        return (grad_sum.at[slot_rows].add(row_grad.astype(jnp.float32)), None)
    moe_grad, _ = lax.scan(backward, jnp.zeros((token_count + 1, features), jnp.float32), (slot_token, slot_gate, gate_matrix, up_matrix, down_matrix))
    input_grad = (resid_grad + moe_grad[:token_count]).astype(jnp.bfloat16)
    return (input_grad, gain_grad)
```

```python
import jax
import jax.numpy as jnp
from jax import lax
from jax.sharding import PartitionSpec as P


def route_ranks(routes, experts):
    flat_ids = routes.reshape(-1)
    onehot = (flat_ids[:, None] == jnp.arange(experts, dtype=jnp.int32)[None, :]).astype(jnp.int32)
    before = jnp.cumsum(onehot, axis=0) - onehot
    return jnp.sum(before * onehot, axis=1).reshape(routes.shape)


def slot_positions(routes, experts, capacity):
    ranks = route_ranks(routes, experts)
    return routes * capacity + ranks


def to_owner(slot_rows, experts, capacity):
    features = slot_rows.shape[1]
    arrived = lax.all_to_all(
        slot_rows.reshape(experts, capacity, features),
        "expert",
        split_axis=0,
        concat_axis=0,
        tiled=True,
    )
    return arrived.reshape(experts * capacity, features)


def to_source(slot_rows, experts, capacity):
    features = slot_rows.shape[1]
    arrived = lax.all_to_all(
        slot_rows.reshape(experts, capacity, features),
        "expert",
        split_axis=0,
        concat_axis=0,
        tiled=True,
    )
    return arrived.reshape(experts * capacity, features)


def selectors(positions, slot_count):
    slot_ids = jnp.arange(slot_count, dtype=jnp.int32)
    return [
        (positions[:, column][:, None] == slot_ids[None, :]).astype(jnp.bfloat16)
        for column in range(positions.shape[1])
    ]


def place_rows(chosen, row_sets):
    placed = lax.dot_general(
        chosen[0], row_sets[0], (((0,), (0,)), ((), ())), preferred_element_type=jnp.float32
    )
    placed = placed + lax.dot_general(
        chosen[1], row_sets[1], (((0,), (0,)), ((), ())), preferred_element_type=jnp.float32
    )
    return placed.astype(jnp.bfloat16)


def project(expert_rows, gate_local, up_local):
    pre_gate = jnp.dot(expert_rows, gate_local, preferred_element_type=jnp.float32)
    pre_up = jnp.dot(expert_rows, up_local, preferred_element_type=jnp.float32)
    return (pre_gate, pre_up)


def shards(tokens, cotangent, routes, route_gates, norm_gain, gate_matrix, up_matrix, down_matrix):
    experts = lax.axis_size("expert")
    token_rows = tokens.shape[0]
    top_routes = routes.shape[1]
    capacity = 2 * token_rows * top_routes // experts
    slot_count = experts * capacity
    gate_local = gate_matrix[0]
    up_local = up_matrix[0]
    down_local = down_matrix[0]
    positions = slot_positions(routes, experts, capacity)
    chosen = selectors(positions, slot_count)
    outgoing = place_rows(chosen, [tokens for column in range(top_routes)])
    expert_rows = to_owner(outgoing, experts, capacity)
    pre_gate, pre_up = project(expert_rows, gate_local, up_local)
    sigmoid_gate = jax.nn.sigmoid(pre_gate)
    hidden = (pre_gate * sigmoid_gate * pre_up).astype(jnp.bfloat16)
    expert_out = lax.dot_general(
        hidden, down_local, (((1,), (1,)), ((), ())), preferred_element_type=jnp.float32
    ).astype(jnp.bfloat16)
    returned = to_source(expert_out, experts, capacity)
    combined = jnp.zeros(tokens.shape, jnp.float32)
    for column in range(top_routes):
        combined = combined + route_gates[:, column : column + 1] * jnp.dot(
            chosen[column], returned, preferred_element_type=jnp.float32
        )
    residual = tokens.astype(jnp.float32) + combined
    inverse_rms = lax.rsqrt(jnp.mean(residual * residual, axis=1, keepdims=True) + 1e-06)
    normed = residual * inverse_rms
    upstream = cotangent.astype(jnp.float32)
    gain_grad = lax.psum_scatter(
        jnp.sum(upstream * normed, axis=0), ("dp", "expert"), scatter_dimension=0, tiled=True
    )
    scaled = upstream * norm_gain[None, :]
    resid_grad = inverse_rms * (scaled - normed * jnp.mean(scaled * normed, axis=1, keepdims=True))
    weighted = [
        (route_gates[:, column : column + 1] * resid_grad).astype(jnp.bfloat16)
        for column in range(top_routes)
    ]
    route_grad = to_owner(place_rows(chosen, weighted), experts, capacity)
    hidden_grad = jnp.dot(route_grad, down_local, preferred_element_type=jnp.float32)
    gate_grad = (
        hidden_grad * pre_up * sigmoid_gate * (1.0 + pre_gate * (1.0 - sigmoid_gate))
    ).astype(jnp.bfloat16)
    up_grad = (hidden_grad * pre_gate * sigmoid_gate).astype(jnp.bfloat16)
    row_grad = lax.dot_general(
        gate_grad, gate_local, (((1,), (1,)), ((), ())), preferred_element_type=jnp.float32
    )
    row_grad = row_grad + lax.dot_general(
        up_grad, up_local, (((1,), (1,)), ((), ())), preferred_element_type=jnp.float32
    )
    back_rows = to_source(row_grad.astype(jnp.bfloat16), experts, capacity)
    moe_grad = jnp.zeros(tokens.shape, jnp.float32)
    for column in range(top_routes):
        moe_grad = moe_grad + jnp.dot(chosen[column], back_rows, preferred_element_type=jnp.float32)
    input_grad = (resid_grad + moe_grad).astype(jnp.bfloat16)
    return (input_grad, gain_grad)


def core_swap(block):
    return lax.ppermute(block, "expert", [(i, i ^ 1) for i in range(8)])


def end_link(block):
    return lax.ppermute(block, "expert", [(i, i ^ 2) for i in range(8)])


def middle_link(block):
    return lax.ppermute(block, "expert", [(2, 4), (3, 5), (4, 2), (5, 3)])


def wide(block):
    return block.astype(jnp.float32)


def narrow(block):
    return block.astype(jnp.bfloat16)


def line_slot(inner, own, parts):
    rows = None
    total = None
    if own is not None:
        near = end_link(own)
        other_mid = middle_link(own)
        other_end = middle_link(near)
    if own is None:
        send = parts[3]
    elif parts is None:
        send = other_mid
    else:
        send = jnp.where(inner, other_mid, parts[3])
    second = end_link(send)
    if own is None:
        send = parts[2]
    elif parts is None:
        send = other_end
    else:
        send = jnp.where(inner, other_end, parts[2])
    third = end_link(send)
    if own is not None:
        rows = jnp.concatenate(
            [own, near, jnp.where(inner, other_mid, second), jnp.where(inner, other_end, third)], axis=0
        )
    if parts is not None:
        far = middle_link(narrow(wide(parts[3]) + wide(second)))
        across = middle_link(narrow(wide(parts[2]) + wide(third)))
        last = end_link(narrow(wide(parts[1]) + wide(far)))
        total = wide(parts[0]) + wide(across) + wide(last)
    return (rows, total)


def matmul(left, right):
    return jnp.dot(left, right, preferred_element_type=jnp.float32)


def matmul_t(left, right):
    return lax.dot_general(left, right, (((1,), (1,)), ((), ())), preferred_element_type=jnp.float32)


def split_rows(array):
    rows = array.shape[0] // 4
    return [array[i * rows : (i + 1) * rows] for i in range(4)]


def forward(rows, scales, weights):
    total = None
    saved = []
    for scale, (gate, up, down) in zip(scales, weights):
        pre_gate = matmul(rows, gate)
        pre_up = matmul(rows, up)
        sigmoid_gate = jax.nn.sigmoid(pre_gate)
        hidden = narrow(scale * (pre_gate * sigmoid_gate * pre_up))
        out = matmul_t(hidden, down)
        total = out if total is None else total + out
        saved.append((pre_gate, pre_up))
    return split_rows(narrow(total)), saved


def backward(rows, scales, weights, saved):
    total = None
    for scale, (gate, up, down), (pre_gate, pre_up) in zip(scales, weights, saved):
        sigmoid_gate = jax.nn.sigmoid(pre_gate)
        hidden_grad = scale * matmul(rows, down)
        gate_grad = narrow(hidden_grad * pre_up * sigmoid_gate * (1.0 + pre_gate * (1.0 - sigmoid_gate)))
        up_grad = narrow(hidden_grad * pre_gate * sigmoid_gate)
        out = matmul_t(gate_grad, gate) + matmul_t(up_grad, up)
        total = out if total is None else total + out
    return split_rows(narrow(total))


def norm(tokens, cotangent, norm_gain, combined):
    residual = wide(tokens) + combined
    inverse_rms = lax.rsqrt(jnp.mean(residual * residual, axis=1, keepdims=True) + 1e-06)
    normed = residual * inverse_rms
    upstream = wide(cotangent)
    gain_part = jnp.sum(upstream * normed, axis=0)
    scaled = upstream * norm_gain[None, :]
    resid_grad = inverse_rms * (scaled - normed * jnp.mean(scaled * normed, axis=1, keepdims=True))
    return resid_grad, gain_part


def halve(total, axis, partner, upper):
    size = total.shape[0] // 2
    low, high = total[:size], total[size:]
    return jnp.where(upper, high, low) + lax.ppermute(jnp.where(upper, low, high), axis, partner)


def sum_gain(total):
    row = lax.axis_index("dp")
    index = lax.axis_index("expert")
    total = halve(total, "dp", [(i, i ^ 2) for i in range(4)], row >= 2)
    total = halve(total, "dp", [(i, i ^ 1) for i in range(4)], row % 2 == 1)
    total = halve(total, "expert", [(i, i ^ 4) for i in range(8)], index >= 4)
    total = halve(total, "expert", [(i, i ^ 2) for i in range(8)], (index // 2) % 2 == 1)
    total = halve(total, "expert", [(i, i ^ 1) for i in range(8)], index % 2 == 1)
    return total


def line_gates(routes, route_gates, chip, core):
    expert_ids = jnp.arange(8, dtype=jnp.int32)
    gates = jnp.sum(
        jnp.where(routes[:, :, None] == expert_ids[None, None, :], route_gates[:, :, None], 0.0), axis=1
    )
    sent = gates.T.reshape(4, 2, gates.shape[0])
    arrived = lax.all_to_all(
        sent, "expert", 0, 0, axis_index_groups=[[0, 2, 4, 6], [1, 3, 5, 7]], tiled=True
    )
    first = chip // 2 * 2
    inner_chip = jnp.where(chip < 2, 2, 1)
    order = jnp.stack([chip, chip ^ 1, inner_chip, 3 * (1 - chip // 2)])
    arrived = arrived[order]
    mine = jnp.where(core == 0, arrived[:, 0], arrived[:, 1])
    other = jnp.where(core == 0, arrived[:, 1], arrived[:, 0])
    return mine, other


def line_shards(tokens, cotangent, routes, route_gates, norm_gain, gate_matrix, up_matrix, down_matrix):
    chunk = tokens.shape[0] // 2
    index = lax.axis_index("expert")
    chip, core = index // 2, index % 2
    inner = (chip == 1) | (chip == 2)
    local = (gate_matrix[0], up_matrix[0], down_matrix[0])
    other = tuple(core_swap(matrix) for matrix in local)
    weights = (local, other)
    gates = line_gates(routes, route_gates, chip, core)
    parts = [slice(0, chunk), slice(chunk, 2 * chunk)]
    scales = [[gate[:, part].reshape(4 * chunk, 1) for gate in gates] for part in parts]
    first, second = parts

    rows_a, _ = line_slot(inner, tokens[first], None)
    out_a, saved_a = forward(rows_a, scales[0], weights)
    rows_b, combined_a = line_slot(inner, tokens[second], out_a)
    grad_a, gain_a = norm(tokens[first], cotangent[first], norm_gain, combined_a)
    out_b, saved_b = forward(rows_b, scales[1], weights)
    rows_a, combined_b = line_slot(inner, narrow(grad_a), out_b)
    grad_b, gain_b = norm(tokens[second], cotangent[second], norm_gain, combined_b)
    gain_grad = sum_gain(gain_a + gain_b)
    back_a = backward(rows_a, scales[0], weights, saved_a)
    rows_b, moe_a = line_slot(inner, narrow(grad_b), back_a)
    back_b = backward(rows_b, scales[1], weights, saved_b)
    _, moe_b = line_slot(inner, None, back_b)
    input_grad = jnp.concatenate([narrow(grad_a + moe_a), narrow(grad_b + moe_b)], axis=0)
    return (input_grad, gain_grad)


def solution(mesh):
    placed = (
        P(("dp", "expert"), None),
        P(("dp", "expert"), None),
        P(("dp", "expert"), None),
        P(("dp", "expert"), None),
        P(),
        P("expert", None, None),
        P("expert", None, None),
        P("expert", None, None),
    )
    body = line_shards if mesh.shape["expert"] == 8 else shards
    return jax.shard_map(
        body,
        mesh=mesh,
        in_specs=placed,
        out_specs=(P(("dp", "expert"), None), P(("dp", "expert"))),
        check_vma=False,
    )
```

```python
import jax
import jax.numpy as jnp
from jax import lax
from jax.sharding import PartitionSpec as P


def route_ranks(routes, experts):
    flat_ids = routes.reshape(-1)
    onehot = (flat_ids[:, None] == jnp.arange(experts, dtype=jnp.int32)[None, :]).astype(jnp.int32)
    before = jnp.cumsum(onehot, axis=0) - onehot
    return jnp.sum(before * onehot, axis=1).reshape(routes.shape)


def slot_positions(routes, experts, capacity):
    ranks = route_ranks(routes, experts)
    return routes * capacity + ranks


def to_owner(slot_rows, experts, capacity):
    features = slot_rows.shape[1]
    arrived = lax.all_to_all(
        slot_rows.reshape(experts, capacity, features),
        "expert",
        split_axis=0,
        concat_axis=0,
        tiled=True,
    )
    return arrived.reshape(experts * capacity, features)


def to_source(slot_rows, experts, capacity):
    features = slot_rows.shape[1]
    arrived = lax.all_to_all(
        slot_rows.reshape(experts, capacity, features),
        "expert",
        split_axis=0,
        concat_axis=0,
        tiled=True,
    )
    return arrived.reshape(experts * capacity, features)


def selectors(positions, slot_count):
    slot_ids = jnp.arange(slot_count, dtype=jnp.int32)
    return [
        (positions[:, column][:, None] == slot_ids[None, :]).astype(jnp.bfloat16)
        for column in range(positions.shape[1])
    ]


def place_rows(chosen, row_sets):
    placed = lax.dot_general(
        chosen[0], row_sets[0], (((0,), (0,)), ((), ())), preferred_element_type=jnp.float32
    )
    placed = placed + lax.dot_general(
        chosen[1], row_sets[1], (((0,), (0,)), ((), ())), preferred_element_type=jnp.float32
    )
    return placed.astype(jnp.bfloat16)


def project(expert_rows, gate_local, up_local):
    pre_gate = jnp.dot(expert_rows, gate_local, preferred_element_type=jnp.float32)
    pre_up = jnp.dot(expert_rows, up_local, preferred_element_type=jnp.float32)
    return (pre_gate, pre_up)


def shards(tokens, cotangent, routes, route_gates, norm_gain, gate_matrix, up_matrix, down_matrix):
    experts = lax.axis_size("expert")
    token_rows = tokens.shape[0]
    top_routes = routes.shape[1]
    capacity = 2 * token_rows * top_routes // experts
    slot_count = experts * capacity
    gate_local = gate_matrix[0]
    up_local = up_matrix[0]
    down_local = down_matrix[0]
    positions = slot_positions(routes, experts, capacity)
    chosen = selectors(positions, slot_count)
    outgoing = place_rows(chosen, [tokens for column in range(top_routes)])
    expert_rows = to_owner(outgoing, experts, capacity)
    pre_gate, pre_up = project(expert_rows, gate_local, up_local)
    sigmoid_gate = jax.nn.sigmoid(pre_gate)
    hidden = (pre_gate * sigmoid_gate * pre_up).astype(jnp.bfloat16)
    expert_out = lax.dot_general(
        hidden, down_local, (((1,), (1,)), ((), ())), preferred_element_type=jnp.float32
    ).astype(jnp.bfloat16)
    returned = to_source(expert_out, experts, capacity)
    combined = jnp.zeros(tokens.shape, jnp.float32)
    for column in range(top_routes):
        combined = combined + route_gates[:, column : column + 1] * jnp.dot(
            chosen[column], returned, preferred_element_type=jnp.float32
        )
    residual = tokens.astype(jnp.float32) + combined
    inverse_rms = lax.rsqrt(jnp.mean(residual * residual, axis=1, keepdims=True) + 1e-06)
    normed = residual * inverse_rms
    upstream = cotangent.astype(jnp.float32)
    gain_grad = lax.psum_scatter(
        jnp.sum(upstream * normed, axis=0), ("dp", "expert"), scatter_dimension=0, tiled=True
    )
    scaled = upstream * norm_gain[None, :]
    resid_grad = inverse_rms * (scaled - normed * jnp.mean(scaled * normed, axis=1, keepdims=True))
    weighted = [
        (route_gates[:, column : column + 1] * resid_grad).astype(jnp.bfloat16)
        for column in range(top_routes)
    ]
    route_grad = to_owner(place_rows(chosen, weighted), experts, capacity)
    hidden_grad = jnp.dot(route_grad, down_local, preferred_element_type=jnp.float32)
    gate_grad = (
        hidden_grad * pre_up * sigmoid_gate * (1.0 + pre_gate * (1.0 - sigmoid_gate))
    ).astype(jnp.bfloat16)
    up_grad = (hidden_grad * pre_gate * sigmoid_gate).astype(jnp.bfloat16)
    row_grad = lax.dot_general(
        gate_grad, gate_local, (((1,), (1,)), ((), ())), preferred_element_type=jnp.float32
    )
    row_grad = row_grad + lax.dot_general(
        up_grad, up_local, (((1,), (1,)), ((), ())), preferred_element_type=jnp.float32
    )
    back_rows = to_source(row_grad.astype(jnp.bfloat16), experts, capacity)
    moe_grad = jnp.zeros(tokens.shape, jnp.float32)
    for column in range(top_routes):
        moe_grad = moe_grad + jnp.dot(chosen[column], back_rows, preferred_element_type=jnp.float32)
    input_grad = (resid_grad + moe_grad).astype(jnp.bfloat16)
    return (input_grad, gain_grad)


def core_swap(block):
    return lax.ppermute(block, "expert", [(i, i ^ 1) for i in range(8)])


def end_link(block):
    return lax.ppermute(block, "expert", [(i, i ^ 2) for i in range(8)])


def middle_link(block):
    return lax.ppermute(block, "expert", [(2, 4), (3, 5), (4, 2), (5, 3)])


def after(value, *others):
    return lax.optimization_barrier((value, *others))[0]


def wide(block):
    return block.astype(jnp.float32)


def narrow(block):
    return block.astype(jnp.bfloat16)


def nothing(block):
    return jnp.minimum(jnp.abs(block[:16, :128]), 0)[0, 0]


def matmul(left, right):
    return jnp.dot(left, right, preferred_element_type=jnp.float32)


def matmul_t(left, right):
    return lax.dot_general(left, right, (((1,), (1,)), ((), ())), preferred_element_type=jnp.float32)


def split_rows(array):
    rows = array.shape[0] // 4
    return [array[i * rows : (i + 1) * rows] for i in range(4)]


def forward(rows, scales, weights):
    total = None
    saved = []
    for scale, (gate, up, down) in zip(scales, weights):
        pre_gate = matmul(rows, gate)
        pre_up = matmul(rows, up)
        sigmoid_gate = jax.nn.sigmoid(pre_gate)
        hidden = narrow(scale * (pre_gate * sigmoid_gate * pre_up))
        out = matmul_t(hidden, down)
        total = out if total is None else total + out
        saved.append((pre_gate, pre_up))
    return split_rows(narrow(total)), saved


def backward(rows, scales, weights, saved):
    total = None
    for scale, (gate, up, down), (pre_gate, pre_up) in zip(scales, weights, saved):
        sigmoid_gate = jax.nn.sigmoid(pre_gate)
        hidden_grad = scale * matmul(rows, down)
        gate_grad = narrow(hidden_grad * pre_up * sigmoid_gate * (1.0 + pre_gate * (1.0 - sigmoid_gate)))
        up_grad = narrow(hidden_grad * pre_gate * sigmoid_gate)
        out = matmul_t(gate_grad, gate) + matmul_t(up_grad, up)
        total = out if total is None else total + out
    return split_rows(narrow(total))


def norm(tokens, cotangent, norm_gain, combined):
    residual = wide(tokens) + combined
    inverse_rms = lax.rsqrt(jnp.mean(residual * residual, axis=1, keepdims=True) + 1e-06)
    normed = residual * inverse_rms
    upstream = wide(cotangent)
    gain_part = jnp.sum(upstream * normed, axis=0)
    scaled = upstream * norm_gain[None, :]
    resid_grad = inverse_rms * (scaled - normed * jnp.mean(scaled * normed, axis=1, keepdims=True))
    return resid_grad, gain_part


def halve(total, axis, partner, upper):
    size = total.shape[0] // 2
    low, high = total[:size], total[size:]
    return jnp.where(upper, high, low) + lax.ppermute(jnp.where(upper, low, high), axis, partner)


def line_gates(routes, route_gates, chip, core):
    expert_ids = jnp.arange(8, dtype=jnp.int32)
    gates = jnp.sum(
        jnp.where(routes[:, :, None] == expert_ids[None, None, :], route_gates[:, :, None], 0.0), axis=1
    )
    sent = gates.T.reshape(4, 2, gates.shape[0])
    arrived = lax.all_to_all(
        sent, "expert", 0, 0, axis_index_groups=[[0, 2, 4, 6], [1, 3, 5, 7]], tiled=True
    )
    inner_chip = jnp.where(chip < 2, 2, 1)
    order = jnp.stack([chip, chip ^ 1, inner_chip, 3 * (1 - chip // 2)])
    arrived = arrived[order]
    return jnp.where(core == 0, arrived, arrived[:, ::-1])


def line_shards(tokens, cotangent, routes, route_gates, norm_gain, gate_matrix, up_matrix, down_matrix):
    chunk = tokens.shape[0] // 2
    index = lax.axis_index("expert")
    chip, core = index // 2, index % 2
    row = lax.axis_index("dp")
    inner = (chip == 1) | (chip == 2)
    local = (gate_matrix[0], up_matrix[0], down_matrix[0])
    other = tuple(core_swap(matrix) for matrix in local)
    weights = (local, other)
    gates = line_gates(routes, route_gates, chip, core)
    first, second = slice(0, chunk), slice(chunk, 2 * chunk)
    scale_a, scale_b = [
        [gates[:, which, part].reshape(4 * chunk, 1) for which in range(2)] for part in (first, second)
    ]

    def gathered(own, near, mid_in, mid_out, end_in, end_out):
        return jnp.concatenate(
            [own, near, jnp.where(inner, mid_in, mid_out), jnp.where(inner, end_in, end_out)], axis=0
        )

    def shared_slot(own, near, mid_in, parts):
        mid_out = end_link(jnp.where(inner, mid_in + nothing(near), parts[3] + nothing(near)))
        end_in = middle_link(near)
        far_sent = narrow(wide(parts[3]) + wide(mid_out))
        far = middle_link(far_sent)
        late = after(parts[2], far_sent)
        end_out = end_link(jnp.where(inner, end_in, late))
        rows = gathered(own, near, mid_in, mid_out, end_in, end_out)
        across = middle_link(narrow(wide(late) + wide(end_out)))
        last = end_link(after(narrow(wide(parts[1]) + wide(far)), end_out))
        return rows, wide(parts[0]) + wide(across) + wide(last)

    own_a, own_b = tokens[first], tokens[second]
    near = end_link(own_a)
    mid_in = middle_link(own_a)
    mid_out = end_link(mid_in)
    end_in = middle_link(near)
    end_out = end_link(after(end_in, mid_out))
    mid_in_b = middle_link(own_b + nothing(end_in))
    near_b = end_link(own_b + nothing(end_out))
    parts_a, saved_a = forward(gathered(own_a, near, mid_in, mid_out, end_in, end_out), scale_a, weights)
    rows_b, combined_a = shared_slot(own_b, near_b, mid_in_b, parts_a)
    grad_a, gain_a = norm(own_a, cotangent[first], norm_gain, combined_a)
    sent_a = narrow(grad_a)
    near_a, mid_in_a = end_link(sent_a), middle_link(sent_a)
    parts_b, saved_b = forward(rows_b, scale_b, weights)
    rows_a, combined_b = shared_slot(sent_a, near_a, mid_in_a, parts_b)
    grad_b, gain_b = norm(own_b, cotangent[second], norm_gain, combined_b)
    sent_b = narrow(grad_b)
    near_b, mid_in_b = end_link(sent_b), middle_link(sent_b)
    gain = gain_a + gain_b
    gain = halve(gain, "dp", [(i, i ^ 2) for i in range(4)], row >= 2)
    gain = halve(gain, "dp", [(i, i ^ 1) for i in range(4)], row % 2 == 1)
    parts_a = backward(rows_a, scale_a, weights, saved_a)
    rows_b, moe_a = shared_slot(sent_b, near_b, mid_in_b, parts_a)
    gain = halve(gain, "expert", [(i, i ^ 4) for i in range(8)], index >= 4)
    gain = halve(gain, "expert", [(i, i ^ 2) for i in range(8)], (index // 2) % 2 == 1)
    parts_b = backward(rows_b, scale_b, weights, saved_b)
    mid_out = end_link(parts_b[3])
    far_sent = narrow(wide(parts_b[3]) + wide(mid_out))
    far = middle_link(far_sent)
    late = after(parts_b[2], far_sent)
    end_out = end_link(late)
    across = middle_link(narrow(wide(late) + wide(end_out)))
    last = end_link(after(narrow(wide(parts_b[1]) + wide(far)), end_out))
    gain = halve(gain, "expert", [(i, i ^ 1) for i in range(8)], core == 1)
    moe_b = wide(parts_b[0]) + wide(across) + wide(last)
    input_grad = jnp.concatenate([narrow(grad_a + moe_a), narrow(grad_b + moe_b)], axis=0)
    return (input_grad, gain)


def solution(mesh):
    placed = (
        P(("dp", "expert"), None),
        P(("dp", "expert"), None),
        P(("dp", "expert"), None),
        P(("dp", "expert"), None),
        P(),
        P("expert", None, None),
        P("expert", None, None),
        P("expert", None, None),
    )
    body = line_shards if mesh.shape["expert"] == 8 else shards
    return jax.shard_map(
        body,
        mesh=mesh,
        in_specs=placed,
        out_specs=(P(("dp", "expert"), None), P(("dp", "expert"))),
        check_vma=False,
    )
```

```python
import jax
import jax.numpy as jnp
from jax import lax
from jax.experimental import pallas as pl
from jax.experimental.pallas import tpu as pltpu
from jax.sharding import PartitionSpec as P

VMEM_LIMIT = 52 * 1024 * 1024
COST = 10**10


def route_ranks(routes, experts):
    flat_ids = routes.reshape(-1)
    onehot = (flat_ids[:, None] == jnp.arange(experts, dtype=jnp.int32)[None, :]).astype(jnp.int32)
    before = jnp.cumsum(onehot, axis=0) - onehot
    return jnp.sum(before * onehot, axis=1).reshape(routes.shape)


def slot_positions(routes, experts, capacity):
    ranks = route_ranks(routes, experts)
    return routes * capacity + ranks


def to_owner(slot_rows, experts, capacity):
    features = slot_rows.shape[1]
    arrived = lax.all_to_all(
        slot_rows.reshape(experts, capacity, features),
        "expert",
        split_axis=0,
        concat_axis=0,
        tiled=True,
    )
    return arrived.reshape(experts * capacity, features)


def to_source(slot_rows, experts, capacity):
    features = slot_rows.shape[1]
    arrived = lax.all_to_all(
        slot_rows.reshape(experts, capacity, features),
        "expert",
        split_axis=0,
        concat_axis=0,
        tiled=True,
    )
    return arrived.reshape(experts * capacity, features)


def selectors(positions, slot_count):
    slot_ids = jnp.arange(slot_count, dtype=jnp.int32)
    return [
        (positions[:, column][:, None] == slot_ids[None, :]).astype(jnp.bfloat16)
        for column in range(positions.shape[1])
    ]


def place_rows(chosen, row_sets):
    placed = lax.dot_general(
        chosen[0], row_sets[0], (((0,), (0,)), ((), ())), preferred_element_type=jnp.float32
    )
    placed = placed + lax.dot_general(
        chosen[1], row_sets[1], (((0,), (0,)), ((), ())), preferred_element_type=jnp.float32
    )
    return placed.astype(jnp.bfloat16)


def project(expert_rows, gate_local, up_local):
    pre_gate = jnp.dot(expert_rows, gate_local, preferred_element_type=jnp.float32)
    pre_up = jnp.dot(expert_rows, up_local, preferred_element_type=jnp.float32)
    return (pre_gate, pre_up)


def shards(tokens, cotangent, routes, route_gates, norm_gain, gate_matrix, up_matrix, down_matrix):
    experts = lax.axis_size("expert")
    token_rows = tokens.shape[0]
    top_routes = routes.shape[1]
    capacity = 2 * token_rows * top_routes // experts
    slot_count = experts * capacity
    gate_local = gate_matrix[0]
    up_local = up_matrix[0]
    down_local = down_matrix[0]
    positions = slot_positions(routes, experts, capacity)
    chosen = selectors(positions, slot_count)
    outgoing = place_rows(chosen, [tokens for column in range(top_routes)])
    expert_rows = to_owner(outgoing, experts, capacity)
    pre_gate, pre_up = project(expert_rows, gate_local, up_local)
    sigmoid_gate = jax.nn.sigmoid(pre_gate)
    hidden = (pre_gate * sigmoid_gate * pre_up).astype(jnp.bfloat16)
    expert_out = lax.dot_general(
        hidden, down_local, (((1,), (1,)), ((), ())), preferred_element_type=jnp.float32
    ).astype(jnp.bfloat16)
    returned = to_source(expert_out, experts, capacity)
    combined = jnp.zeros(tokens.shape, jnp.float32)
    for column in range(top_routes):
        combined = combined + route_gates[:, column : column + 1] * jnp.dot(
            chosen[column], returned, preferred_element_type=jnp.float32
        )
    residual = tokens.astype(jnp.float32) + combined
    inverse_rms = lax.rsqrt(jnp.mean(residual * residual, axis=1, keepdims=True) + 1e-06)
    normed = residual * inverse_rms
    upstream = cotangent.astype(jnp.float32)
    gain_grad = lax.psum_scatter(
        jnp.sum(upstream * normed, axis=0), ("dp", "expert"), scatter_dimension=0, tiled=True
    )
    scaled = upstream * norm_gain[None, :]
    resid_grad = inverse_rms * (scaled - normed * jnp.mean(scaled * normed, axis=1, keepdims=True))
    weighted = [
        (route_gates[:, column : column + 1] * resid_grad).astype(jnp.bfloat16)
        for column in range(top_routes)
    ]
    route_grad = to_owner(place_rows(chosen, weighted), experts, capacity)
    hidden_grad = jnp.dot(route_grad, down_local, preferred_element_type=jnp.float32)
    gate_grad = (
        hidden_grad * pre_up * sigmoid_gate * (1.0 + pre_gate * (1.0 - sigmoid_gate))
    ).astype(jnp.bfloat16)
    up_grad = (hidden_grad * pre_gate * sigmoid_gate).astype(jnp.bfloat16)
    row_grad = lax.dot_general(
        gate_grad, gate_local, (((1,), (1,)), ((), ())), preferred_element_type=jnp.float32
    )
    row_grad = row_grad + lax.dot_general(
        up_grad, up_local, (((1,), (1,)), ((), ())), preferred_element_type=jnp.float32
    )
    back_rows = to_source(row_grad.astype(jnp.bfloat16), experts, capacity)
    moe_grad = jnp.zeros(tokens.shape, jnp.float32)
    for column in range(top_routes):
        moe_grad = moe_grad + jnp.dot(chosen[column], back_rows, preferred_element_type=jnp.float32)
    input_grad = (resid_grad + moe_grad).astype(jnp.bfloat16)
    return (input_grad, gain_grad)


TILE = 768
RING = 2
WIDE = 2048


def gather_rows(inner_ref, own, near, mid_in, mid_out, end_in, end_out, rows):
    size = own.shape[0]
    rows[0:size] = own[...]
    rows[size : 2 * size] = near[...]

    @pl.when(inner_ref[0] == 1)
    def _():
        rows[2 * size : 3 * size] = mid_in[...]
        rows[3 * size : 4 * size] = end_in[...]

    @pl.when(inner_ref[0] == 0)
    def _():
        rows[2 * size : 3 * size] = mid_out[...]
        rows[3 * size : 4 * size] = end_out[...]


def column_copies(order, ring, sems):
    units = order[0].shape[1]
    tiles = [(i, t) for i in range(0, len(order), 2) for t in range(units // TILE)]
    jobs = [(order[i + k], t) for i, t in tiles for k in range(2)]
    return [
        pltpu.make_async_copy(
            matrix.at[:, pl.ds(t * TILE, TILE)], ring.at[n % RING], sems.at[n % RING]
        )
        for n, (matrix, t) in enumerate(jobs)
    ]


def row_copies(order, held, sems):
    spans = order[0].shape[0] // WIDE
    return [
        [
            pltpu.make_async_copy(
                matrix.at[pl.ds(span * WIDE, WIDE), :],
                held.at[span * len(order) + i],
                sems.at[span * len(order) + i],
            )
            for i, matrix in enumerate(order)
        ]
        for span in range(spans)
    ]


def dot_t(left, right):
    return lax.dot_general(left, right, (((1,), (1,)), ((), ())), preferred_element_type=jnp.float32)


def stream(columns, spans, use):
    pending = columns[RING:] + [copy for span in spans for copy in span]
    for copy in columns[:RING]:
        copy.start()
    for n, copy in enumerate(columns):
        copy.wait()
        use(n)
        ahead = 1 if n + RING < len(columns) else len(pending)
        for later in pending[:ahead]:
            later.start()
        pending = pending[ahead:]


def send_back(lefts, spans, held, parts):
    size = parts[0].shape[0]
    for s, span in enumerate(spans):
        total = None
        for i, copy in enumerate(span):
            copy.wait()
            out = dot_t(lefts[i], held[s * len(span) + i])
            total = out if total is None else total + out
        for p, part in enumerate(parts):
            part[:, s * WIDE : (s + 1) * WIDE] = total[p * size : (p + 1) * size].astype(part.dtype)


def forward_kernel(inner_ref, *refs):
    blocks, (scale, *weights), refs = refs[:6], refs[6:13], refs[13:]
    parts, (gate_out, up_out), refs = refs[:4], refs[4:6], refs[6:]
    rows, hidden, ring, held, ring_sems, held_sems = refs
    gate, up, down, gate_b, up_b, down_b = weights
    columns = column_copies([gate, up, gate_b, up_b], ring, ring_sems)
    spans = row_copies([down, down_b], held, held_sems)
    tiles = len(columns) // 4

    def use(n):
        if n == 0:
            gather_rows(inner_ref, *blocks, rows)
        step = n // 2
        pre = jnp.dot(rows[...], ring[n % RING], preferred_element_type=jnp.float32)
        if n % 2 == 0:
            gate_out[step] = pre
        else:
            up_out[step] = pre
            pre_gate = gate_out[step]
            value = scale[step // tiles] * (pre_gate * jax.nn.sigmoid(pre_gate) * pre)
            hidden[step // tiles, :, (step % tiles) * TILE : (step % tiles + 1) * TILE] = value.astype(
                hidden.dtype
            )

    stream(columns, spans, use)
    send_back([hidden[0], hidden[1]], spans, held, parts)


def backward_kernel(inner_ref, *refs):
    blocks, (gate_in, up_in, scale, *weights), refs = refs[:6], refs[6:15], refs[15:]
    parts, (rows, grads, ring, held, ring_sems, held_sems) = refs[:4], refs[4:]
    gate, up, down, gate_b, up_b, down_b = weights
    columns = column_copies([down, down_b], ring, ring_sems)
    spans = row_copies([gate, up, gate_b, up_b], held, held_sems)
    tiles = len(columns) // 2

    def use(n):
        if n == 0:
            gather_rows(inner_ref, *blocks, rows)
        expert, tile = n % 2, n // 2
        step = expert * tiles + tile
        pre_gate, pre_up = gate_in[step], up_in[step]
        sigmoid_gate = jax.nn.sigmoid(pre_gate)
        hidden_grad = scale[expert] * jnp.dot(
            rows[...], ring[n % RING], preferred_element_type=jnp.float32
        )
        gate_grad = hidden_grad * pre_up * sigmoid_gate * (1.0 + pre_gate * (1.0 - sigmoid_gate))
        up_grad = hidden_grad * pre_gate * sigmoid_gate
        span = slice(tile * TILE, (tile + 1) * TILE)
        grads[2 * expert, :, span] = gate_grad.astype(grads.dtype)
        grads[2 * expert + 1, :, span] = up_grad.astype(grads.dtype)

    stream(columns, spans, use)
    send_back([grads[i] for i in range(4)], spans, held, parts)


def expert_call(kernel, inner, blocks, saved, scale, weights):
    rows, features = blocks[0].shape
    units = weights[0].shape[1]
    tiles = units // TILE
    part = jax.ShapeDtypeStruct((rows, features), jnp.bfloat16)
    pre = jax.ShapeDtypeStruct((2 * tiles, 4 * rows, TILE), jnp.float32)
    vmem, hbm = pl.BlockSpec(memory_space=pltpu.VMEM), pl.BlockSpec(memory_space=pl.ANY)
    outs = [part] * 4 + ([] if saved else [pre] * 2)
    kept = 4 if saved else 2
    held = kept * (features // WIDE)
    return pl.pallas_call(
        kernel,
        out_shape=outs,
        in_specs=[pl.BlockSpec(memory_space=pltpu.SMEM)] + [vmem] * (7 + len(saved)) + [hbm] * 6,
        out_specs=[vmem] * len(outs),
        scratch_shapes=[
            pltpu.VMEM((4 * rows, features), jnp.bfloat16),
            pltpu.VMEM((kept, 4 * rows, units), jnp.bfloat16),
            pltpu.VMEM((RING, features, TILE), jnp.bfloat16),
            pltpu.VMEM((held, WIDE, units), jnp.bfloat16),
            pltpu.SemaphoreType.DMA((RING,)),
            pltpu.SemaphoreType.DMA((held,)),
        ],
        compiler_params=pltpu.CompilerParams(vmem_limit_bytes=VMEM_LIMIT),
        cost_estimate=pl.CostEstimate(flops=COST, bytes_accessed=0, transcendentals=0),
    )(inner, *blocks, *saved, scale, *weights)


def core_swap(block):
    return lax.ppermute(block, "expert", [(i, i ^ 1) for i in range(8)])


def end_link(block):
    return lax.ppermute(block, "expert", [(i, i ^ 2) for i in range(8)])


def middle_link(block):
    return lax.ppermute(block, "expert", [(2, 4), (3, 5), (4, 2), (5, 3)])


def after(value, *others):
    return lax.optimization_barrier((value, *others))[0]


def wide(block):
    return block.astype(jnp.float32)


def narrow(block):
    return block.astype(jnp.bfloat16)


def nothing(block):
    return jnp.minimum(jnp.abs(block[:16, :128]), 0)[0, 0]


def matmul(left, right):
    return jnp.dot(left, right, preferred_element_type=jnp.float32)


def matmul_t(left, right):
    return lax.dot_general(left, right, (((1,), (1,)), ((), ())), preferred_element_type=jnp.float32)


def split_rows(array):
    rows = array.shape[0] // 4
    return [array[i * rows : (i + 1) * rows] for i in range(4)]


def forward(rows, scales, weights):
    total = None
    saved = []
    for scale, (gate, up, down) in zip(scales, weights):
        pre_gate = matmul(rows, gate)
        pre_up = matmul(rows, up)
        sigmoid_gate = jax.nn.sigmoid(pre_gate)
        hidden = narrow(scale * (pre_gate * sigmoid_gate * pre_up))
        out = matmul_t(hidden, down)
        total = out if total is None else total + out
        saved.append((pre_gate, pre_up))
    return split_rows(narrow(total)), saved


def backward(rows, scales, weights, saved):
    total = None
    for scale, (gate, up, down), (pre_gate, pre_up) in zip(scales, weights, saved):
        sigmoid_gate = jax.nn.sigmoid(pre_gate)
        hidden_grad = scale * matmul(rows, down)
        gate_grad = narrow(hidden_grad * pre_up * sigmoid_gate * (1.0 + pre_gate * (1.0 - sigmoid_gate)))
        up_grad = narrow(hidden_grad * pre_gate * sigmoid_gate)
        out = matmul_t(gate_grad, gate) + matmul_t(up_grad, up)
        total = out if total is None else total + out
    return split_rows(narrow(total))


def norm(tokens, cotangent, norm_gain, combined):
    residual = wide(tokens) + combined
    inverse_rms = lax.rsqrt(jnp.mean(residual * residual, axis=1, keepdims=True) + 1e-06)
    normed = residual * inverse_rms
    upstream = wide(cotangent)
    gain_part = jnp.sum(upstream * normed, axis=0)
    scaled = upstream * norm_gain[None, :]
    resid_grad = inverse_rms * (scaled - normed * jnp.mean(scaled * normed, axis=1, keepdims=True))
    return resid_grad, gain_part


def halve(total, axis, partner, upper):
    size = total.shape[0] // 2
    low, high = total[:size], total[size:]
    return jnp.where(upper, high, low) + lax.ppermute(jnp.where(upper, low, high), axis, partner)


def line_gates(routes, route_gates, chip, core):
    expert_ids = jnp.arange(8, dtype=jnp.int32)
    gates = jnp.sum(
        jnp.where(routes[:, :, None] == expert_ids[None, None, :], route_gates[:, :, None], 0.0), axis=1
    )
    sent = gates.T.reshape(4, 2, gates.shape[0])
    arrived = lax.all_to_all(
        sent, "expert", 0, 0, axis_index_groups=[[0, 2, 4, 6], [1, 3, 5, 7]], tiled=True
    )
    inner_chip = jnp.where(chip < 2, 2, 1)
    order = jnp.stack([chip, chip ^ 1, inner_chip, 3 * (1 - chip // 2)])
    arrived = arrived[order]
    return jnp.where(core == 0, arrived, arrived[:, ::-1])


def line_shards(tokens, cotangent, routes, route_gates, norm_gain, gate_matrix, up_matrix, down_matrix):
    chunk = tokens.shape[0] // 2
    index = lax.axis_index("expert")
    chip, core = index // 2, index % 2
    row = lax.axis_index("dp")
    inner = (chip == 1) | (chip == 2)
    local = (gate_matrix[0], up_matrix[0], down_matrix[0])
    other = tuple(core_swap(matrix) for matrix in local)
    weights = (local, other)
    gates = line_gates(routes, route_gates, chip, core)
    first, second = slice(0, chunk), slice(chunk, 2 * chunk)
    scale_a, scale_b = [
        [gates[:, which, part].reshape(4 * chunk, 1) for which in range(2)] for part in (first, second)
    ]

    def gathered(own, near, mid_in, mid_out, end_in, end_out):
        return jnp.concatenate(
            [own, near, jnp.where(inner, mid_in, mid_out), jnp.where(inner, end_in, end_out)], axis=0
        )

    def shared_slot(own, near, mid_in, parts, ready):
        mid_out = end_link(jnp.where(inner, mid_in + ready, parts[3] + ready))
        end_in = middle_link(near)
        far_sent = narrow(wide(parts[3]) + wide(mid_out))
        far = middle_link(far_sent)
        late = after(parts[2], far_sent)
        end_out = end_link(jnp.where(inner, end_in, late))
        blocks = [own, near, mid_in, mid_out, end_in, end_out]
        across = middle_link(narrow(wide(late) + wide(end_out)))
        last = end_link(after(narrow(wide(parts[1]) + wide(far)), end_out))
        return blocks, wide(parts[0]) + wide(across) + wide(last)

    own_a, own_b = tokens[first], tokens[second]
    near = end_link(own_a)
    mid_in = middle_link(own_a)
    mid_out = end_link(mid_in)
    end_in = middle_link(near)
    end_out = end_link(after(end_in, mid_out))
    mid_in_b = middle_link(own_b + nothing(end_in))
    near_b = end_link(own_b + nothing(end_out))
    flag = inner.astype(jnp.int32).reshape(1)
    flat = local + other
    blocks = [own_a, near, mid_in, mid_out, end_in, end_out]
    outs = expert_call(forward_kernel, flag, blocks, [], jnp.stack(scale_a), flat)
    parts_a = list(outs[:4])
    saved_a = [(outs[4][e], outs[5][e]) for e in range(2)]
    rows_b, combined_a = shared_slot(own_b, near_b, mid_in_b, parts_a, 0)
    grad_a, gain_a = norm(own_a, cotangent[first], norm_gain, combined_a)
    sent_a = narrow(grad_a)
    near_a, mid_in_a = end_link(sent_a), middle_link(sent_a)
    parts_b, saved_b = forward(gathered(*rows_b), scale_b, weights)
    rows_a, combined_b = shared_slot(sent_a, near_a, mid_in_a, parts_b, nothing(near_a))
    grad_b, gain_b = norm(own_b, cotangent[second], norm_gain, combined_b)
    sent_b = narrow(grad_b)
    near_b, mid_in_b = end_link(sent_b), middle_link(sent_b)
    gain = gain_a + gain_b
    gain = halve(gain, "dp", [(i, i ^ 2) for i in range(4)], row >= 2)
    gain = halve(gain, "dp", [(i, i ^ 1) for i in range(4)], row % 2 == 1)
    parts_a = backward(gathered(*rows_a), scale_a, weights, saved_a)
    rows_b, moe_a = shared_slot(sent_b, near_b, mid_in_b, parts_a, nothing(near_b))
    gain = halve(gain, "expert", [(i, i ^ 4) for i in range(8)], index >= 4)
    gain = halve(gain, "expert", [(i, i ^ 2) for i in range(8)], (index // 2) % 2 == 1)
    saved_b = [jnp.stack([saved_b[e][i] for e in range(2)]) for i in range(2)]
    parts_b = list(expert_call(backward_kernel, flag, rows_b, saved_b, jnp.stack(scale_b), flat))
    mid_out = end_link(parts_b[3])
    far_sent = narrow(wide(parts_b[3]) + wide(mid_out))
    far = middle_link(far_sent)
    late = after(parts_b[2], far_sent)
    end_out = end_link(late)
    across = middle_link(narrow(wide(late) + wide(end_out)))
    last = end_link(after(narrow(wide(parts_b[1]) + wide(far)), end_out))
    gain = halve(gain, "expert", [(i, i ^ 1) for i in range(8)], core == 1)
    moe_b = wide(parts_b[0]) + wide(across) + wide(last)
    input_grad = jnp.concatenate([narrow(grad_a + moe_a), narrow(grad_b + moe_b)], axis=0)
    return (input_grad, gain)


def solution(mesh):
    placed = (
        P(("dp", "expert"), None),
        P(("dp", "expert"), None),
        P(("dp", "expert"), None),
        P(("dp", "expert"), None),
        P(),
        P("expert", None, None),
        P("expert", None, None),
        P("expert", None, None),
    )
    body = line_shards if mesh.shape["expert"] == 8 else shards
    return jax.shard_map(
        body,
        mesh=mesh,
        in_specs=placed,
        out_specs=(P(("dp", "expert"), None), P(("dp", "expert"))),
        check_vma=False,
    )
```

```python
import jax
import jax.numpy as jnp
from jax import lax
from jax.experimental import pallas as pl
from jax.experimental.pallas import tpu as pltpu
from jax.sharding import PartitionSpec as P

VMEM_LIMIT = 52 * 1024 * 1024
COST = 10**10


def route_ranks(routes, experts):
    flat_ids = routes.reshape(-1)
    onehot = (flat_ids[:, None] == jnp.arange(experts, dtype=jnp.int32)[None, :]).astype(jnp.int32)
    before = jnp.cumsum(onehot, axis=0) - onehot
    return jnp.sum(before * onehot, axis=1).reshape(routes.shape)


def slot_positions(routes, experts, capacity):
    ranks = route_ranks(routes, experts)
    return routes * capacity + ranks


def to_owner(slot_rows, experts, capacity):
    features = slot_rows.shape[1]
    arrived = lax.all_to_all(
        slot_rows.reshape(experts, capacity, features),
        "expert",
        split_axis=0,
        concat_axis=0,
        tiled=True,
    )
    return arrived.reshape(experts * capacity, features)


def to_source(slot_rows, experts, capacity):
    features = slot_rows.shape[1]
    arrived = lax.all_to_all(
        slot_rows.reshape(experts, capacity, features),
        "expert",
        split_axis=0,
        concat_axis=0,
        tiled=True,
    )
    return arrived.reshape(experts * capacity, features)


def selectors(positions, slot_count):
    slot_ids = jnp.arange(slot_count, dtype=jnp.int32)
    return [
        (positions[:, column][:, None] == slot_ids[None, :]).astype(jnp.bfloat16)
        for column in range(positions.shape[1])
    ]


def place_rows(chosen, row_sets):
    placed = lax.dot_general(
        chosen[0], row_sets[0], (((0,), (0,)), ((), ())), preferred_element_type=jnp.float32
    )
    placed = placed + lax.dot_general(
        chosen[1], row_sets[1], (((0,), (0,)), ((), ())), preferred_element_type=jnp.float32
    )
    return placed.astype(jnp.bfloat16)


def project(expert_rows, gate_local, up_local):
    pre_gate = jnp.dot(expert_rows, gate_local, preferred_element_type=jnp.float32)
    pre_up = jnp.dot(expert_rows, up_local, preferred_element_type=jnp.float32)
    return (pre_gate, pre_up)


def shards(tokens, cotangent, routes, route_gates, norm_gain, gate_matrix, up_matrix, down_matrix):
    experts = lax.axis_size("expert")
    token_rows = tokens.shape[0]
    top_routes = routes.shape[1]
    capacity = 2 * token_rows * top_routes // experts
    slot_count = experts * capacity
    gate_local = gate_matrix[0]
    up_local = up_matrix[0]
    down_local = down_matrix[0]
    positions = slot_positions(routes, experts, capacity)
    chosen = selectors(positions, slot_count)
    outgoing = place_rows(chosen, [tokens for column in range(top_routes)])
    expert_rows = to_owner(outgoing, experts, capacity)
    pre_gate, pre_up = project(expert_rows, gate_local, up_local)
    sigmoid_gate = jax.nn.sigmoid(pre_gate)
    hidden = (pre_gate * sigmoid_gate * pre_up).astype(jnp.bfloat16)
    expert_out = lax.dot_general(
        hidden, down_local, (((1,), (1,)), ((), ())), preferred_element_type=jnp.float32
    ).astype(jnp.bfloat16)
    returned = to_source(expert_out, experts, capacity)
    combined = jnp.zeros(tokens.shape, jnp.float32)
    for column in range(top_routes):
        combined = combined + route_gates[:, column : column + 1] * jnp.dot(
            chosen[column], returned, preferred_element_type=jnp.float32
        )
    residual = tokens.astype(jnp.float32) + combined
    inverse_rms = lax.rsqrt(jnp.mean(residual * residual, axis=1, keepdims=True) + 1e-06)
    normed = residual * inverse_rms
    upstream = cotangent.astype(jnp.float32)
    gain_grad = lax.psum_scatter(
        jnp.sum(upstream * normed, axis=0), ("dp", "expert"), scatter_dimension=0, tiled=True
    )
    scaled = upstream * norm_gain[None, :]
    resid_grad = inverse_rms * (scaled - normed * jnp.mean(scaled * normed, axis=1, keepdims=True))
    weighted = [
        (route_gates[:, column : column + 1] * resid_grad).astype(jnp.bfloat16)
        for column in range(top_routes)
    ]
    route_grad = to_owner(place_rows(chosen, weighted), experts, capacity)
    hidden_grad = jnp.dot(route_grad, down_local, preferred_element_type=jnp.float32)
    gate_grad = (
        hidden_grad * pre_up * sigmoid_gate * (1.0 + pre_gate * (1.0 - sigmoid_gate))
    ).astype(jnp.bfloat16)
    up_grad = (hidden_grad * pre_gate * sigmoid_gate).astype(jnp.bfloat16)
    row_grad = lax.dot_general(
        gate_grad, gate_local, (((1,), (1,)), ((), ())), preferred_element_type=jnp.float32
    )
    row_grad = row_grad + lax.dot_general(
        up_grad, up_local, (((1,), (1,)), ((), ())), preferred_element_type=jnp.float32
    )
    back_rows = to_source(row_grad.astype(jnp.bfloat16), experts, capacity)
    moe_grad = jnp.zeros(tokens.shape, jnp.float32)
    for column in range(top_routes):
        moe_grad = moe_grad + jnp.dot(chosen[column], back_rows, preferred_element_type=jnp.float32)
    input_grad = (resid_grad + moe_grad).astype(jnp.bfloat16)
    return (input_grad, gain_grad)


TILE = 768
RING = 2
WIDE = 2048


def gather_rows(inner_ref, own, near, mid_in, mid_out, end_in, end_out, rows):
    size = own.shape[0]
    rows[0:size] = own[...]
    rows[size : 2 * size] = near[...]

    @pl.when(inner_ref[0] == 1)
    def _():
        rows[2 * size : 3 * size] = mid_in[...]
        rows[3 * size : 4 * size] = end_in[...]

    @pl.when(inner_ref[0] == 0)
    def _():
        rows[2 * size : 3 * size] = mid_out[...]
        rows[3 * size : 4 * size] = end_out[...]


def column_copies(order, ring, sems):
    units = order[0].shape[1]
    tiles = [(i, t) for i in range(0, len(order), 2) for t in range(units // TILE)]
    jobs = [(order[i + k], t) for i, t in tiles for k in range(2)]
    return [
        pltpu.make_async_copy(
            matrix.at[:, pl.ds(t * TILE, TILE)], ring.at[n % RING], sems.at[n % RING]
        )
        for n, (matrix, t) in enumerate(jobs)
    ]


def row_copies(order, held, sems):
    spans = order[0].shape[0] // WIDE
    return [
        [
            pltpu.make_async_copy(
                matrix.at[pl.ds(span * WIDE, WIDE), :],
                held.at[span * len(order) + i],
                sems.at[span * len(order) + i],
            )
            for i, matrix in enumerate(order)
        ]
        for span in range(spans)
    ]


def dot_t(left, right):
    return lax.dot_general(left, right, (((1,), (1,)), ((), ())), preferred_element_type=jnp.float32)


def stream(columns, spans, use):
    for copy in columns[:RING]:
        copy.start()
    for n, copy in enumerate(columns):
        copy.wait()
        if n == 0:
            for later in (copy for span in spans for copy in span):
                later.start()
        use(n)
        if n + RING < len(columns):
            columns[n + RING].start()


def send_back(lefts, spans, held, parts):
    size = parts[0].shape[0]
    for s, span in enumerate(spans):
        total = None
        for i, copy in enumerate(span):
            copy.wait()
            out = dot_t(lefts[i], held[s * len(span) + i])
            total = out if total is None else total + out
        for p, part in enumerate(parts):
            part[:, s * WIDE : (s + 1) * WIDE] = total[p * size : (p + 1) * size].astype(part.dtype)


def forward_kernel(inner_ref, *refs):
    blocks, (scale, *weights), refs = refs[:6], refs[6:13], refs[13:]
    parts, (gate_out, up_out), refs = refs[:4], refs[4:6], refs[6:]
    rows, hidden, ring, held, ring_sems, held_sems = refs
    gate, up, down, gate_b, up_b, down_b = weights
    columns = column_copies([gate, up, gate_b, up_b], ring, ring_sems)
    spans = row_copies([down, down_b], held, held_sems)
    tiles = len(columns) // 4

    def use(n):
        if n == 0:
            gather_rows(inner_ref, *blocks, rows)
        step = n // 2
        pre = jnp.dot(rows[...], ring[n % RING], preferred_element_type=jnp.float32)
        if n % 2 == 0:
            gate_out[step] = pre
        else:
            up_out[step] = pre
            pre_gate = gate_out[step]
            value = scale[step // tiles] * (pre_gate * jax.nn.sigmoid(pre_gate) * pre)
            hidden[step // tiles, :, (step % tiles) * TILE : (step % tiles + 1) * TILE] = value.astype(
                hidden.dtype
            )

    stream(columns, spans, use)
    send_back([hidden[0], hidden[1]], spans, held, parts)


def backward_kernel(inner_ref, *refs):
    blocks, (gate_in, up_in, scale, *weights), refs = refs[:6], refs[6:15], refs[15:]
    parts, (rows, grads, ring, held, ring_sems, held_sems) = refs[:4], refs[4:]
    gate, up, down, gate_b, up_b, down_b = weights
    columns = column_copies([down, down_b], ring, ring_sems)
    spans = row_copies([gate, up, gate_b, up_b], held, held_sems)
    tiles = len(columns) // 2

    def use(n):
        if n == 0:
            gather_rows(inner_ref, *blocks, rows)
        expert, tile = n % 2, n // 2
        step = expert * tiles + tile
        pre_gate, pre_up = gate_in[step], up_in[step]
        sigmoid_gate = jax.nn.sigmoid(pre_gate)
        hidden_grad = scale[expert] * jnp.dot(
            rows[...], ring[n % RING], preferred_element_type=jnp.float32
        )
        gate_grad = hidden_grad * pre_up * sigmoid_gate * (1.0 + pre_gate * (1.0 - sigmoid_gate))
        up_grad = hidden_grad * pre_gate * sigmoid_gate
        span = slice(tile * TILE, (tile + 1) * TILE)
        grads[2 * expert, :, span] = gate_grad.astype(grads.dtype)
        grads[2 * expert + 1, :, span] = up_grad.astype(grads.dtype)

    stream(columns, spans, use)
    send_back([grads[i] for i in range(4)], spans, held, parts)


def expert_call(kernel, inner, blocks, saved, scale, weights):
    rows, features = blocks[0].shape
    units = weights[0].shape[1]
    tiles = units // TILE
    part = jax.ShapeDtypeStruct((rows, features), jnp.bfloat16)
    pre = jax.ShapeDtypeStruct((2 * tiles, 4 * rows, TILE), jnp.float32)
    vmem, hbm = pl.BlockSpec(memory_space=pltpu.VMEM), pl.BlockSpec(memory_space=pl.ANY)
    outs = [part] * 4 + ([] if saved else [pre] * 2)
    kept = 4 if saved else 2
    held = kept * (features // WIDE)
    return pl.pallas_call(
        kernel,
        out_shape=outs,
        in_specs=[pl.BlockSpec(memory_space=pltpu.SMEM)] + [vmem] * (7 + len(saved)) + [hbm] * 6,
        out_specs=[vmem] * len(outs),
        scratch_shapes=[
            pltpu.VMEM((4 * rows, features), jnp.bfloat16),
            pltpu.VMEM((kept, 4 * rows, units), jnp.bfloat16),
            pltpu.VMEM((RING, features, TILE), jnp.bfloat16),
            pltpu.VMEM((held, WIDE, units), jnp.bfloat16),
            pltpu.SemaphoreType.DMA((RING,)),
            pltpu.SemaphoreType.DMA((held,)),
        ],
        compiler_params=pltpu.CompilerParams(vmem_limit_bytes=VMEM_LIMIT),
        cost_estimate=pl.CostEstimate(flops=COST, bytes_accessed=0, transcendentals=0),
    )(inner, *blocks, *saved, scale, *weights)


def core_swap(block):
    return lax.ppermute(block, "expert", [(i, i ^ 1) for i in range(8)])


def end_link(block):
    return lax.ppermute(block, "expert", [(i, i ^ 2) for i in range(8)])


def middle_link(block):
    return lax.ppermute(block, "expert", [(2, 4), (3, 5), (4, 2), (5, 3)])


def after(value, *others):
    return lax.optimization_barrier((value, *others))[0]


def wide(block):
    return block.astype(jnp.float32)


def narrow(block):
    return block.astype(jnp.bfloat16)


def nothing(block):
    return jnp.minimum(jnp.abs(block[:16, :128]), 0)[0, 0]


def matmul(left, right):
    return jnp.dot(left, right, preferred_element_type=jnp.float32)


def matmul_t(left, right):
    return lax.dot_general(left, right, (((1,), (1,)), ((), ())), preferred_element_type=jnp.float32)


def split_rows(array):
    rows = array.shape[0] // 4
    return [array[i * rows : (i + 1) * rows] for i in range(4)]


def forward(rows, scales, weights):
    total = None
    saved = []
    for scale, (gate, up, down) in zip(scales, weights):
        pre_gate = matmul(rows, gate)
        pre_up = matmul(rows, up)
        sigmoid_gate = jax.nn.sigmoid(pre_gate)
        hidden = narrow(scale * (pre_gate * sigmoid_gate * pre_up))
        out = matmul_t(hidden, down)
        total = out if total is None else total + out
        saved.append((pre_gate, pre_up))
    return split_rows(narrow(total)), saved


def backward(rows, scales, weights, saved):
    total = None
    for scale, (gate, up, down), (pre_gate, pre_up) in zip(scales, weights, saved):
        sigmoid_gate = jax.nn.sigmoid(pre_gate)
        hidden_grad = scale * matmul(rows, down)
        gate_grad = narrow(hidden_grad * pre_up * sigmoid_gate * (1.0 + pre_gate * (1.0 - sigmoid_gate)))
        up_grad = narrow(hidden_grad * pre_gate * sigmoid_gate)
        out = matmul_t(gate_grad, gate) + matmul_t(up_grad, up)
        total = out if total is None else total + out
    return split_rows(narrow(total))


def norm(tokens, cotangent, norm_gain, combined):
    residual = wide(tokens) + combined
    inverse_rms = lax.rsqrt(jnp.mean(residual * residual, axis=1, keepdims=True) + 1e-06)
    normed = residual * inverse_rms
    upstream = wide(cotangent)
    gain_part = jnp.sum(upstream * normed, axis=0)
    scaled = upstream * norm_gain[None, :]
    resid_grad = inverse_rms * (scaled - normed * jnp.mean(scaled * normed, axis=1, keepdims=True))
    return resid_grad, gain_part


def halve(total, axis, partner, upper):
    size = total.shape[0] // 2
    low, high = total[:size], total[size:]
    return jnp.where(upper, high, low) + lax.ppermute(jnp.where(upper, low, high), axis, partner)


def line_gates(routes, route_gates, chip, core):
    expert_ids = jnp.arange(8, dtype=jnp.int32)
    gates = jnp.sum(
        jnp.where(routes[:, :, None] == expert_ids[None, None, :], route_gates[:, :, None], 0.0), axis=1
    )
    sent = gates.T.reshape(4, 2, gates.shape[0])
    arrived = lax.all_to_all(
        sent, "expert", 0, 0, axis_index_groups=[[0, 2, 4, 6], [1, 3, 5, 7]], tiled=True
    )
    inner_chip = jnp.where(chip < 2, 2, 1)
    order = jnp.stack([chip, chip ^ 1, inner_chip, 3 * (1 - chip // 2)])
    arrived = arrived[order]
    return jnp.where(core == 0, arrived, arrived[:, ::-1])


def line_shards(tokens, cotangent, routes, route_gates, norm_gain, gate_matrix, up_matrix, down_matrix):
    chunk = tokens.shape[0] // 2
    index = lax.axis_index("expert")
    chip, core = index // 2, index % 2
    row = lax.axis_index("dp")
    inner = (chip == 1) | (chip == 2)
    local = (gate_matrix[0], up_matrix[0], down_matrix[0])
    other = tuple(core_swap(matrix) for matrix in local)
    weights = (local, other)
    gates = line_gates(routes, route_gates, chip, core)
    first, second = slice(0, chunk), slice(chunk, 2 * chunk)
    scale_a, scale_b = [
        [gates[:, which, part].reshape(4 * chunk, 1) for which in range(2)] for part in (first, second)
    ]

    def gathered(own, near, mid_in, mid_out, end_in, end_out):
        return jnp.concatenate(
            [own, near, jnp.where(inner, mid_in, mid_out), jnp.where(inner, end_in, end_out)], axis=0
        )

    def shared_slot(own, near, mid_in, parts, ready):
        mid_out = end_link(jnp.where(inner, mid_in + ready, parts[3] + ready))
        end_in = middle_link(near)
        far_sent = narrow(wide(parts[3]) + wide(mid_out))
        far = middle_link(far_sent)
        late = after(parts[2], far_sent)
        end_out = end_link(jnp.where(inner, end_in, late))
        blocks = [own, near, mid_in, mid_out, end_in, end_out]
        across = middle_link(narrow(wide(late) + wide(end_out)))
        last = end_link(after(narrow(wide(parts[1]) + wide(far)), end_out))
        return blocks, wide(parts[0]) + wide(across) + wide(last)

    own_a, own_b = tokens[first], tokens[second]
    near = end_link(own_a)
    mid_in = middle_link(own_a)
    mid_out = end_link(mid_in)
    end_in = middle_link(near)
    end_out = end_link(after(end_in, mid_out))
    mid_in_b = middle_link(own_b + nothing(end_in))
    near_b = end_link(own_b + nothing(end_out))
    flag = inner.astype(jnp.int32).reshape(1)
    flat = local + other
    blocks = [own_a, near, mid_in, mid_out, end_in, end_out]
    outs = expert_call(forward_kernel, flag, blocks, [], jnp.stack(scale_a), flat)
    parts_a = list(outs[:4])
    saved_a = [(outs[4][e], outs[5][e]) for e in range(2)]
    rows_b, combined_a = shared_slot(own_b, near_b, mid_in_b, parts_a, 0)
    grad_a, gain_a = norm(own_a, cotangent[first], norm_gain, combined_a)
    sent_a = narrow(grad_a)
    near_a, mid_in_a = end_link(sent_a), middle_link(sent_a)
    parts_b, saved_b = forward(gathered(*rows_b), scale_b, weights)
    rows_a, combined_b = shared_slot(sent_a, near_a, mid_in_a, parts_b, nothing(near_a))
    grad_b, gain_b = norm(own_b, cotangent[second], norm_gain, combined_b)
    sent_b = narrow(grad_b)
    near_b, mid_in_b = end_link(sent_b), middle_link(sent_b)
    gain = gain_a + gain_b
    gain = halve(gain, "dp", [(i, i ^ 2) for i in range(4)], row >= 2)
    gain = halve(gain, "dp", [(i, i ^ 1) for i in range(4)], row % 2 == 1)
    parts_a = backward(gathered(*rows_a), scale_a, weights, saved_a)
    rows_b, moe_a = shared_slot(sent_b, near_b, mid_in_b, parts_a, nothing(near_b))
    gain = halve(gain, "expert", [(i, i ^ 4) for i in range(8)], index >= 4)
    gain = halve(gain, "expert", [(i, i ^ 2) for i in range(8)], (index // 2) % 2 == 1)
    saved_b = [jnp.stack([saved_b[e][i] for e in range(2)]) for i in range(2)]
    parts_b = list(expert_call(backward_kernel, flag, rows_b, saved_b, jnp.stack(scale_b), flat))
    mid_out = end_link(parts_b[3])
    far_sent = narrow(wide(parts_b[3]) + wide(mid_out))
    far = middle_link(far_sent)
    late = after(parts_b[2], far_sent)
    end_out = end_link(late)
    across = middle_link(narrow(wide(late) + wide(end_out)))
    last = end_link(after(narrow(wide(parts_b[1]) + wide(far)), end_out))
    gain = halve(gain, "expert", [(i, i ^ 1) for i in range(8)], core == 1)
    moe_b = wide(parts_b[0]) + wide(across) + wide(last)
    input_grad = jnp.concatenate([narrow(grad_a + moe_a), narrow(grad_b + moe_b)], axis=0)
    return (input_grad, gain)


def solution(mesh):
    placed = (
        P(("dp", "expert"), None),
        P(("dp", "expert"), None),
        P(("dp", "expert"), None),
        P(("dp", "expert"), None),
        P(),
        P("expert", None, None),
        P("expert", None, None),
        P("expert", None, None),
    )
    body = line_shards if mesh.shape["expert"] == 8 else shards
    return jax.shard_map(
        body,
        mesh=mesh,
        in_specs=placed,
        out_specs=(P(("dp", "expert"), None), P(("dp", "expert"))),
        check_vma=False,
    )
```
